128 devices in a mesh: section: 2 (over core), seq: 4 (over z), fsdp: 16 (over y, x).
Axes of the slice: x: 4, y: 4, z: 4, core: 2. Of those that a mesh axis runs over, the one named last changes fastest.
Arguments:
- edges: bfloat16 [2, 2, 16, 608, 768], P('section', None, 'fsdp', 'seq'), may hold values from -6 to 6
- lengths: int32 [4], replicated, may hold values from 1 to 152, 576 in all
- qkv_weight: bfloat16 [2, 768, 2304], P('section', 'fsdp'), may hold values from -0.21875 to 0.21875
- out_weight: bfloat16 [2, 768, 768], P('section', 'fsdp'), may hold values from -3 to 3
- up_weight: bfloat16 [2, 768, 3072], P('section', 'fsdp'), may hold values from -0.21875 to 0.21875
- down_weight: bfloat16 [2, 3072, 768], P('section', None, 'fsdp'), may hold values from -0.109375 to 0.109375
- gains: bfloat16 [2, 2, 768], P('section', None, 'fsdp'), may hold values from 0.099609375 to 1.8984375
- biases: bfloat16 [2, 6, 768], P('section', None, 'fsdp'), may hold values from -0.59765625 to 0.59765625
- hidden_bias: bfloat16 [2, 3072], P('section'), may hold values from -1.796875 to 1.796875
Outputs:
- boundary: float32 [2, 2, 16, 608, 768], P('section', None, 'fsdp', 'seq')
- qkv_grad: float32 [2, 768, 2304], P('section', ('seq', 'fsdp'))
- out_grad: float32 [2, 768, 768], P('section', ('seq', 'fsdp'))
- up_grad: float32 [2, 768, 3072], P('section', ('seq', 'fsdp'))
- down_grad: float32 [2, 3072, 768], P('section', None, ('seq', 'fsdp'))
- gains_grad: float32 [2, 2, 768], P('section', None, ('seq', 'fsdp'))
- biases_grad: float32 [2, 4, 768], P('section', None, ('seq', 'fsdp'))
- value_bias_grad: float32 [2, 2, 768], P('section', None, ('seq', 'fsdp'))
- hidden_bias_grad: float32 [2, 3072], P('section')
The draws below stay inside these ranges and needn't reach their ends.
Inputs may be any that keep to these rules, and one draw needn't show every extreme that they name: lengths[s] live tokens stand first in sequence shard s; they sum to 576 and one shard is full.
All inputs are finite; a program needn't handle non-finite values.
Results may differ from the reference program's by a relative error of at most 0.019.
Values may be sent and summed in bfloat16 or wider, within the bound.
A program may use at most 384 MiB of HBM per device.

```python
import math
import jax
import jax.numpy as jnp
import numpy as np
from jax import lax

D = 768
HEADS = 12
HDIM = 64
FF = 3072
SLOT = 152
MICRO = 2
TOK = 608
SEQ_LEN = 576
IMAGES = 16
N_SEQ = 4


def shard_levels(key, shape, pieces, low, top_value):
    level = 1.0
    for axis_at, shards_of in pieces:
        steps = jax.random.uniform(jax.random.fold_in(jax.random.fold_in(key, 6), axis_at), (shards_of,), jnp.float32, low / len(pieces), top_value / len(pieces))
        level = level * jnp.repeat(jnp.exp(steps), shape[axis_at] // shards_of).reshape((-1,) + (1,) * (len(shape) - 1 - axis_at))
    return level


def profile(number_of, total, most, skew):
    weights = [(1 << 20) // math.isqrt(rank ** skew) + 1 for rank in range(2, number_of + 1)]
    surplus, counts = total - most - (number_of - 1), [1] * (number_of - 1)
    while surplus > 0:
        movable = [i for i in range(number_of - 1) if counts[i] < most]
        pool, remaining = sum([weights[i] for i in movable]), surplus
        for i in movable:
            addition = min(most - counts[i], max(1, remaining * weights[i] // pool), surplus)
            counts[i] = counts[i] + addition
            surplus = surplus - addition
    return np.array([most] + counts)


def ragged(rng, amount, total, reach, lean):
    if amount == 2:
        one = jax.random.randint(rng, (), max(1, total - reach), min(reach, total - 1) + 1)
        return jnp.stack([one, total - one])
    tallies = jnp.asarray(profile(amount, total, reach, lean), jnp.int32)
    couples = (amount - 1) // 2
    source_of, taker = tallies[1:1 + 2 * couples:2], tallies[2:2 + 2 * couples:2]
    room = jnp.minimum(source_of - 1, reach - taker)
    moved = jax.random.randint(jax.random.fold_in(rng, 1), (couples,), 0, 1 << 20) % (room + 1)
    tallies = tallies.at[1:1 + 2 * couples:2].set(source_of - moved).at[2:2 + 2 * couples:2].set(taker + moved)
    return tallies[jax.random.permutation(jax.random.fold_in(rng, 2), amount)]


def scatter_about(stream_key, dims, width, limit, cuts=(), kind=jnp.bfloat16):
    drawn = jax.random.normal(stream_key, dims, jnp.float32) * width
    if len(cuts) > 0:
        drawn = shard_levels(stream_key, dims, cuts, -0.22, 0.18) * drawn
    return jnp.clip(drawn, min=-limit, max=limit).astype(kind)


def setup_inputs(seed: int = 0) -> dict:
    keys = jax.random.split(jax.random.key(seed), 10)
    return {
        "edges": scatter_about(keys[0], (2, MICRO, IMAGES, TOK, D), 1.0, 6.0, ((0, 2), (2, 16), (3, 4))),
        "lengths": ragged(keys[1], N_SEQ, SEQ_LEN, SLOT, 0).astype(jnp.int32),
        "qkv_weight": scatter_about(keys[2], (2, D, 3 * D), D ** -0.5, 0.21875, ((0, 2), (1, 16))),
        "out_weight": scatter_about(keys[3], (2, D, D), (max(3 * D // SEQ_LEN, 1)) ** -0.5, 3.0, ((0, 2), (1, 16))),
        "up_weight": scatter_about(keys[4], (2, D, FF), D ** -0.5, 0.21875, ((0, 2), (1, 16))),
        "down_weight": scatter_about(keys[5], (2, FF, D), FF ** -0.5, 0.109375, ((0, 2), (2, 16))),
        "gains": jnp.clip(1.0 + 0.18 * jax.random.normal(keys[6], (2, 2, D), jnp.float32), 0.099609375, 1.8984375).astype(jnp.bfloat16),
        "biases": scatter_about(keys[7], (2, 6, D), 0.1, 0.59765625, ((0, 2), (2, 16))),
        "hidden_bias": scatter_about(keys[8], (2, FF), 0.3, 1.796875, ((0, 2),)),
    }


@jax.custom_vjp
def low(v):
    return lax.optimization_barrier(v.astype(jnp.bfloat16)).astype(jnp.float32)

@jax.custom_vjp
def low_back(v):
    return v

def low_keep(v):
    return (low(v), None)

def low_pass(kept, grad):
    return (grad,)

def back_keep(v):
    return (v, None)

def back_low(kept, grad):
    return (low(grad),)
low.defvjp(low_keep, low_pass)
low_back.defvjp(back_keep, back_low)
EPSILON = 1e-06
HIGHEST = lax.Precision.HIGHEST

def product(left, right):
    return jnp.dot(left, right, precision=HIGHEST, preferred_element_type=jnp.float32)

def norm_rows(values, gain, shift):
    center = values - lax.optimization_barrier(jnp.mean(values, axis=-1, keepdims=True))
    spread = lax.optimization_barrier(jnp.mean(center * center, axis=-1, keepdims=True))
    return center * lax.rsqrt(spread + EPSILON) * gain + shift

def residual_block(weights, layer_in, live_rows, key_mask):
    qkv_part, out_part, up_part, down_part, gain_rows, bias_rows, hidden_shift = weights
    length = layer_in.shape[0]
    normed_a = low(norm_rows(layer_in, gain_rows[0], bias_rows[0]))
    projected = product(normed_a, qkv_part)
    query_t = low_back(low(projected[:, :D] + bias_rows[1]))
    key_t = low_back(low(projected[:, D:2 * D]))
    value_t = low_back(low(projected[:, 2 * D:] + bias_rows[2]))
    query_h = query_t.reshape(length, HEADS, HDIM)
    key_h = key_t.reshape(length, HEADS, HDIM)
    value_h = value_t.reshape(length, HEADS, HDIM)
    scores = jnp.einsum('tnh,snh->nts', query_h, key_h, precision=HIGHEST) * HDIM ** (-0.5)
    scores = low_back(scores) + key_mask[None, None, :]
    softmax_w = jax.nn.softmax(scores, axis=-1)
    mixed = jnp.einsum('nts,snh->tnh', low(softmax_w), value_h, precision=HIGHEST)
    mixed = low_back(low(mixed.reshape(length, D)))
    attended = low_back(product(mixed, out_part) + bias_rows[3])
    middle = layer_in + attended
    normed_b = low(norm_rows(middle, gain_rows[1], bias_rows[4]))
    hidden_pre = low_back(product(normed_b, up_part) + hidden_shift)
    hidden = low(jax.nn.gelu(hidden_pre, approximate=True))
    branch = low_back(product(hidden, down_part) + bias_rows[5])
    return live_rows * (middle + branch)

def reference(edges, lengths, qkv_weight, out_weight, up_weight, down_weight, gains, biases, hidden_bias):
    length = N_SEQ * SLOT
    position = jnp.arange(length, dtype=jnp.int32)
    owner_shard = position // SLOT
    shards = jnp.arange(N_SEQ, dtype=jnp.int32)
    shard_limit = lax.optimization_barrier(jnp.sum(jnp.where(owner_shard[:, None] == shards[None, :], lengths[None, :], 0), axis=1))
    live_mask = position % SLOT < shard_limit
    live_rows = jnp.where(live_mask, 1.0, 0.0).astype(jnp.float32)[:, None]
    key_mask = jnp.where(live_mask, 0.0, -1000000000.0).astype(jnp.float32)
    images = edges[0].astype(jnp.float32).reshape(MICRO * IMAGES, length, D)
    cotangent = edges[1].astype(jnp.float32).reshape(MICRO * IMAGES, length, D)
    stacked = [array_in.astype(jnp.float32) for array_in in (qkv_weight, out_weight, up_weight, down_weight, gains, biases, hidden_bias)]
    first_set = tuple((array_in[0] for array_in in stacked))
    second_set = tuple((array_in[1] for array_in in stacked))

    def forward(first_w, second_w, inputs):

        def per_image(image):
            passed = low_back(low(residual_block(first_w, image, live_rows, key_mask)))
            return residual_block(second_w, passed, live_rows, key_mask)
        return lax.map(jax.checkpoint(per_image), inputs)
    outputs, pullback = jax.vjp(forward, first_set, second_set, images)
    lower_grad, upper_grad, image_grad = pullback(cotangent)
    boundary = jnp.stack([image_grad, outputs]).reshape(2, MICRO, IMAGES, length, D)
    grads = [jnp.stack([lower_one, upper_one]) for lower_one, upper_one in zip(lower_grad, upper_grad)]
    bias_all = grads[5]
    bias_rest = jnp.stack([bias_all[:, 1], bias_all[:, 3], bias_all[:, 4], bias_all[:, 5]], axis=1)
    bias_value = jnp.stack([bias_all[:, 0], bias_all[:, 2]], axis=1)
    return (boundary, grads[0], grads[1], grads[2], grads[3], grads[4], bias_rest, bias_value, grads[6])
```

```python
import jax
import jax.numpy as jnp
import numpy as np
from jax import lax
from jax.experimental import pallas as pl
from jax.experimental.pallas import tpu as pltpu
from jax.sharding import PartitionSpec as P

MESH = pl.DeviceIdType.MESH
F32 = jnp.float32
BF16 = jnp.bfloat16

D = 768
HALF = 384
FF = 3072
FH = 1536
SLOT = 152
SLOTP = 160
TOK = 576
TOKP = 640
CH = 288
SHARD = 48
EPSILON = 1e-06
SCALE = 0.125
VMEM_BYTES = 63 * 1024 * 1024

W_VEC = 1152
W_O = 1280
W_U = 1664
W_MINE = 1920
W_SHARE = 640
W_V = 3200
W_ALL = 4736
G_U = 1536
G_O = 3072
G_P = 3456
G_ALL = 4608

GATHER_SETS = (
    ("y", 0, 384, 256),
    ("x", 640, 384, 256),
    ("y", 1280, 128, 256),
    ("x", 1664, 128, 128),
    ("y", 1920, 128, 128),
    ("x", 2176, 128, 256),
    ("y", 3200, 256, 256),
    ("x", 3712, 256, 128),
    ("y", 4096, 128, 128),
    ("x", 4352, 128, 256),
    ("y", 3072, 128, 128),
    ("x", 3328, 256, 128),
)
HELP_SETS = (10, 11)
W_HELP = 4096
G_HELP = 3072
HELP = 640
SHARED_SETS = (4, 5)
SCATTER_SETS = (
    ("x", 0, 128, 128),
    ("y", 256, 128, 128),
    ("x", 1536, 384, 384),
    ("y", 2304, 384, 384),
    ("y", 3072, 128, 256),
    ("y", 3456, 128, 128),
    ("x", 3712, 128, 0),
    ("x", 3840, 128, 256),
    ("x", 4224, 128, 128),
    ("y", 4480, 128, 0),
    ("x", 512, 128, 128),
    ("y", 768, 128, 128),
)
V_SHARE = 512
(
    A, F, Z, WZ, H, WH, CHUNK, VEC, HEADS, ENTER, GVS, GVW, GVO, PA, GU, GO, GP, R, DIST, G1, ROWS, SMX, SMY,
    SMZ, PROJ, AT, OUT, WIDE, NAR, SH, MID, PB, EN,
) = range(33)
GATHER_ORDER = (
    (A, 11, 0), (A, 10, 0), (A, 2, 0), (A, 5, 0), (A, 1, 0), (A, 4, 0), (A, 6, 0), (A, 10, 1), (A, 0, 0), (A, 8, 0),
    (A, 11, 1), (A, 4, 1), (A, 3, 0), (A, 5, 1), (A, 2, 1), (A, 10, 2), (H, 10, 0), (A, 9, 0), (A, 6, 1), (A, 11, 2),
    (A, 5, 2), (A, 1, 1), (H, 11, 0), (A, 4, 2), (A, 10, 3), (A, 3, 1), (A, 9, 1), (A, 8, 1), (A, 7, 0), (H, 10, 1),
    (A, 2, 2), (A, 11, 3), (Z, 5, 0), (F, 10), (A, 0, 1), (A, 4, 3), (H, 11, 1), (A, 5, 3), (A, 3, 2), (Z, 5, 1),
    (A, 7, 1), (A, 1, 2), (A, 6, 2), (F, 4), (F, 5), (A, 8, 2), (A, 7, 2), (F, 11), (H, 11, 2), (A, 2, 3), (Z, 4, 1),
    (H, 10, 2), (Z, 4, 2), (A, 0, 2), (A, 9, 2), (Z, 4, 0), (A, 1, 3), (CHUNK,), (A, 6, 3), (A, 8, 3), (A, 3, 3),
    (Z, 5, 2), (A, 0, 3), (A, 7, 3), (A, 9, 3), (F, 1), (VEC,), (F, 0),
)
GATHER_WAITS = (
    (F, 2), (HEADS,), (WZ, 4), (WZ, 5), (F, 3), (F, 6), (F, 7), (F, 8), (F, 9),
)
FORWARD_ORDER = (
    (A, 4, 0), (A, 0, 0), (A, 1, 0), (A, 5, 0), (A, 2, 0), (A, 3, 0), (A, 4, 1), (A, 7, 0), (A, 1, 1), (A, 0, 1),
    (A, 5, 1), (A, 2, 1), (A, 3, 1), (A, 6, 0), (A, 4, 2), (A, 1, 2), (Z, 4, 0), (A, 5, 2), (Z, 5, 0), (A, 0, 2),
    (A, 6, 1), (A, 4, 3), (Z, 4, 1), (A, 2, 2), (A, 7, 1), (A, 0, 3), (F, 4), (Z, 4, 2), (A, 1, 3), (A, 5, 3),
    (Z, 5, 1), (CHUNK,), (A, 3, 2), (A, 2, 3), (A, 6, 2), (A, 7, 2), (F, 1), (VEC,), (ENTER,), (F, 5), (Z, 5, 2),
    (F, 0), (PROJ,), (AT, 0), (AT, 1), (F, 2), (HEADS,), (A, 3, 3), (AT, 2), (A, 6, 3), (A, 7, 3), (OUT,), (WZ, 4),
    (WZ, 5), (F, 3), (WIDE, 0), (WIDE, 1), (F, 6), (F, 7), (WH,), (NAR,),
)
BACKWARD_ORDER = (
    (SH, 0), (G1,), (GVS,), (R, 0, 0), (R, 1, 0), (SH, 1), (GU, 0), (R, 2, 0), (GU, 1), (R, 3, 0), (GVO,), (MID, 0),
    (R, 1, 1), (R, 0, 1), (MID, 1), (AT, 0), (R, 2, 1), (GP, 0), (R, 3, 1), (AT, 1), (AT, 2), (GP, 2), (R, 8, 0),
    (R, 6, 0), (PB, 0), (R, 9, 0), (GVW,), (GO,), (GP, 1), (R, 4, 0), (PB, 1), (R, 0, 2), (R, 7, 0), (R, 5, 0),
    (PA, 0), (EN, 0), (R, 1, 2), (R, 8, 1), (R, 9, 1), (R, 6, 1), (R, 10, 0), (EN, 1), (R, 4, 1), (SMX,), (R, 7, 1),
    (PA, 1), (R, 11, 0), (R, 5, 1), (R, 4, 2), (R, 8, 2), (R, 6, 2), (R, 9, 2), (R, 10, 1), (R, 11, 1), (R, 9, 3),
    (R, 7, 2), (R, 5, 2), (R, 3, 2), (R, 2, 2), (R, 4, 3), (R, 8, 3), (ROWS,), (R, 10, 2), (R, 6, 3), (R, 9, 4),
    (SMY,), (R, 11, 2), (R, 7, 3), (R, 5, 3), (R, 3, 3), (R, 2, 3), (R, 1, 3), (R, 4, 4), (R, 10, 3), (R, 11, 3),
    (R, 0, 3), (R, 8, 4), (R, 7, 4), (R, 5, 4), (R, 6, 4), (SMZ,), (DIST, 2), (R, 3, 4), (R, 2, 4), (DIST, 1),
    (R, 11, 4), (R, 10, 4), (R, 1, 4), (R, 0, 4), (DIST, 0),
)
SUM_ORDER = (
    (GP, 0), (R, 5, 0), (GU, 0), (R, 2, 0), (GVO,), (GVS,), (R, 1, 0), (GU, 1), (R, 6, 0), (GP, 1), (R, 3, 0),
    (GP, 2), (R, 7, 0), (GO,), (R, 0, 0), (GVW,), (R, 4, 0), (R, 9, 0), (R, 2, 1), (SMX,), (R, 5, 1), (R, 0, 1),
    (R, 3, 1), (PA, 0), (R, 1, 1), (R, 9, 1), (R, 10, 0), (R, 6, 1), (R, 8, 0), (R, 2, 2), (R, 3, 2), (R, 10, 1),
    (PA, 1), (R, 11, 0), (R, 4, 1), (SMY,), (R, 7, 1), (R, 5, 2), (R, 11, 1), (R, 0, 2), (R, 1, 2), (R, 10, 2),
    (R, 6, 2), (R, 8, 1), (R, 7, 2), (R, 3, 3), (ROWS,), (R, 2, 3), (R, 11, 2), (R, 4, 2), (R, 9, 2), (R, 5, 3),
    (R, 8, 2), (R, 1, 3), (R, 6, 3), (R, 0, 3), (R, 10, 3), (R, 7, 3), (R, 11, 3), (R, 3, 4), (R, 9, 3), (R, 2, 4),
    (R, 4, 3), (R, 8, 3), (DIST, 1), (SMZ,), (R, 10, 4), (R, 0, 4), (R, 1, 4), (R, 11, 4), (DIST, 0), (R, 9, 4),
    (R, 5, 4), (R, 8, 4), (R, 6, 4), (R, 7, 4), (R, 4, 4), (DIST, 2),
)
OTHER = {"x": "y", "y": "x"}

NN = (((1,), (0,)), ((), ()))
NT = (((1,), (1,)), ((), ()))
TN = (((0,), (0,)), ((), ()))


def dot(left, right, dims=NN):
    return lax.dot_general(left, right, dims, preferred_element_type=F32)


def mod4(value):
    return lax.rem(value + 4, 4)


def center_rows(values):
    center = values - jnp.mean(values, axis=-1, keepdims=True)
    spread = jnp.mean(center * center, axis=-1, keepdims=True)
    return center, lax.rsqrt(spread + EPSILON)


def norm_back(grad, unit, scale, gain):
    scaled = grad * gain
    first = jnp.mean(scaled, axis=-1, keepdims=True)
    second = jnp.mean(scaled * unit, axis=-1, keepdims=True)
    return scale * (scaled - first - unit * second)


def columns(first, count):
    return pl.ds(first if isinstance(first, int) else pl.multiple_of(first, 128), count)


def rows_of(i):
    return pl.ds(pl.multiple_of(i * CH, 16), CH)


def add_to(ref, index, value):
    ref[index] = (ref[index].astype(F32) + value).astype(ref.dtype)


class Kernel:
    def __init__(self, refs):
        self.__dict__.update(refs)
        self.taken = 0
        self.core = lax.axis_index("section")
        self.z = lax.axis_index("seq")
        f = lax.axis_index("fsdp")
        self.x, self.y = lax.rem(f, 4), f // 4
        self.role = self.z // 2
        self.part = lax.rem(self.z, 2)
        self.image = self.z + self.role * (3 - 2 * self.z)
        self.sibling = (1 - self.core, self.z, f)
        self.partner = (self.core, 3 - self.z, f)
        self.twin = (self.core, self.z + 1 - 2 * self.part, f)
        self.f = f

    def take(self, count=1):
        first = self.taken
        self.taken = first + count
        return first

    def near(self, axis, step):
        if axis == "x":
            return (self.core, self.z, self.y * 4 + mod4(self.x + step))
        return (self.core, self.z, mod4(self.y + step) * 4 + self.x)

    def at(self, axis, step):
        return mod4((self.x if axis == "x" else self.y) + step)

    def remote(self, src, dst, send, recv, device):
        return pltpu.make_async_remote_copy(
            src_ref=src,
            dst_ref=dst,
            send_sem=self.send.at[send],
            recv_sem=self.recv.at[recv],
            device_id=device,
            device_id_type=MESH,
        )

    def local(self, src, dst, recv):
        return pltpu.make_async_copy(src, dst, self.recv.at[recv])

    def signal(self, device):
        pl.semaphore_signal(
            pltpu.get_barrier_semaphore(), inc=1, device_id=device, device_id_type=MESH
        )

    def greet(self):
        for step in (1, 2, 3):
            self.signal(self.near("x", step))
            self.signal(self.near("y", step))
            self.signal((self.core, mod4(self.z + step), self.f))
            self.signal((1 - self.core, mod4(self.z + step), self.f))
        self.signal(self.sibling)

    def greeted(self):
        pl.semaphore_wait(pltpu.get_barrier_semaphore(), 13)

    def prepare(self):
        row = lax.broadcasted_iota(jnp.int32, (TOK, 1), 0)
        place, start = row, 0
        for s in range(4):
            place = jnp.where(row >= start, row - start + s * SLOTP, place)
            start = start + self.lengths[s]
        lane = lax.broadcasted_iota(jnp.int32, (TOK, TOKP), 1)
        self.sel[...] = jnp.where(lane == place, 1.0, 0.0).astype(BF16)
        self.linv[...] = jnp.ones_like(self.linv)
        self.square[...] = jnp.zeros_like(self.square)
        self.square[0:2, 0:SHARD] = self.gains[0].astype(F32)
        self.square[2:8, 0:SHARD] = self.biases[0].astype(F32)
        self.vshard[...] = self.square[...].T[:SHARD, :].astype(BF16)
        self.dist[...] = jnp.zeros_like(self.dist)
        self.chunks[:, SLOT:, :] = jnp.zeros((4, SLOTP - SLOT, D), BF16)
        self.hsource[...] = jnp.broadcast_to(self.hidden[...].astype(F32), (8, FF))

    def zero_tails(self):
        for ref in (self.abuf, self.bbuf, self.qkvt, self.g, self.gz, self.dr, self.mail, self.dm, self.dqkv):
            ref[TOK:, :] = jnp.zeros((TOKP - TOK, ref.shape[1]), ref.dtype)

    def perm_copy(self):
        return self.local(self.order, self.perm, self.perm_sem)

    def chunk_pair(self, m):
        zd, cc = m + self.core * (3 - 2 * m), lax.rem(self.z, 2)
        here = (self.core == cc) & (self.z == zd)
        src, dst = self.edges.at[m], self.slabs.at[self.z]
        return here, src, dst, self.chunk_sem + m, self.chunk_sem + self.z, (cc, zd, self.f)

    def chunk_send(self):
        for m in range(2):
            self.push(*self.chunk_pair(m))

    def chunk_on(self, k, of):
        at = of + 2 * k
        return self.remote(self.slabs.at[at], self.slabs.at[at], self.chunk_sem + 2 + k, self.chunk_sem + at, self.sibling)

    def chunk_wait(self):
        for k in range(2):
            at = self.core + 2 * k
            here = (self.core == self.role) & (self.z == at)
            self.got(here, self.edges.at[0], self.slabs.at[at], self.chunk_sem + at)
            self.chunk_on(k, self.core).start()
        for k in range(2):
            self.chunk_on(k, 1 - self.core).wait_recv()
        for k in range(2):
            self.chunk_on(k, self.core).wait_send()
        for m in range(2):
            self.sent(*self.chunk_pair(m))

        for zs in range(4):
            self.chunks[zs, :SLOT, :] = self.slabs[zs].reshape(SLOT, D)
        rows = dot(self.sel[...], self.chunks[...].reshape(TOKP, D)).astype(BF16)

        @pl.when(self.role == 0)
        def _():
            self.xin[...] = rows

        @pl.when(self.role == 1)
        def _():
            self.dr[:TOK, :] = rows

    def shard_pieces(self, group, half):
        def cols(first, count):
            return pl.ds(pl.multiple_of(first + half * count, 128), count)

        mine = self.w.at[self.y, self.x]

        def here(first, count):
            return mine.at[:, pl.ds(first, count)]

        if group == 0:
            return [
                (self.qkv.at[0, :, pl.ds(pl.multiple_of(D * t + 128 * j + half * HALF, 128), 128)], here(HALF * j + 128 * t, 128))
                for j in range(3)
                for t in range(3)
            ] + [(self.vshard, here(W_VEC, 128)), (self.hsource.at[:, cols(0, FH)], self.hbuf)]
        if group == 1:
            return [(self.outw.at[0, :, cols(0, HALF)], here(W_O, HALF))]
        if group == 2:
            own = W_SHARE * self.part
            source = pl.ds(pl.multiple_of(half * FH + W_MINE - W_U + own, 128), W_SHARE)
            return [
                (self.up.at[0, :, columns(half * FH, W_MINE - W_U)], here(W_U, W_MINE - W_U)),
                (self.up.at[0, :, source], mine.at[:, columns(W_MINE + own, W_SHARE)]),
            ]
        if group == 3:
            return [(self.down.at[0, :, columns(half * FH, W_HELP - W_V)], here(W_V, W_HELP - W_V))]
        help_source = self.down.at[0, :, columns(half * FH + W_HELP - W_V, HELP)]
        if group == 4:
            return [(help_source, here(W_HELP, HELP))]
        return [(help_source, self.gw.at[self.y, self.x, :, pl.ds(G_HELP, HELP)])]

    def shard_far(self, group):
        first = self.shard_sem + (0, 11, 12, 14, 15, 16)[group]
        return [
            self.remote(src, dst, first + n, first + n, self.sibling)
            for n, (src, dst) in enumerate(self.shard_pieces(group, 1 - self.core))
        ]

    def shard_near(self, group):
        first = self.shard_sem + (0, 11, 12, 14, 15, 16)[group]
        return [
            self.local(src, dst, first + n)
            for n, (src, dst) in enumerate(self.shard_pieces(group, self.core))
        ]

    def shard_start(self):
        @pl.when(self.core == self.role)
        def _():
            for group in range(4):
                self.shard_go(group)

        @pl.when((self.core == self.role) & (self.role == 1))
        def _():
            self.shard_go(4)

        @pl.when((self.core != self.role) & (self.role == 1))
        def _():
            self.shard_go(5)

    def shard_go(self, group):
        for copy in self.shard_far(group) + self.shard_near(group):
            copy.start()

    def shard_wait(self, group):
        holds = (self.core != self.role) if group == 5 else (self.core == self.role)

        @pl.when(holds)
        def _():
            for copy in self.shard_near(group):
                copy.wait()
            for copy in self.shard_far(group):
                copy.wait_send()

        @pl.when(jnp.logical_not(holds))
        def _():
            for copy in self.shard_far(group):
                copy.wait_recv()

    def line(self, ref, axis, step, first, count):
        at, cols = self.at(axis, step), columns(first, count)
        if axis == "x":
            return ref.at[self.y, at, :, cols]
        return ref.at[at, self.x, :, cols]

    def sheet(self, ref, axis, step, first, count):
        at, cols = self.at(axis, step), columns(first, count)
        if axis == "x":
            return ref.at[:, at, :, cols]
        return ref.at[at, :, :, cols]

    def spread(self, n, stage, incoming=False):
        axis, first, n1, n2 = GATHER_SETS[n]
        if n in SHARED_SETS:
            first = first + W_SHARE * self.part
        view, ref = (self.line if stage < 2 else self.sheet), (self.gw if n in HELP_SETS else self.w)
        axis = axis if stage < 2 else OTHER[axis]
        sem = self.gather_sem + 8 * n + 2 * stage
        if stage % 2 == 0:
            left, right = ((-1, 1) if incoming else (0, 0))
            blocks = [view(ref, axis, left, first, n1 + n2), view(ref, axis, right, first, n1 + n2)]
        else:
            left, right = ((2, 2) if incoming else (-1, 1))
            blocks = [view(ref, axis, left, first, n1)]
            if n2:
                blocks.append(view(ref, axis, right, first + n1, n2))
        return [
            self.remote(block, block, sem + n, sem + n, self.near(axis, (1, -1)[n]))
            for n, block in enumerate(blocks)
        ]

    def handed(self, n, k, half):
        axis, first, n1, n2 = GATHER_SETS[n]
        sheet = self.sheet(self.w, OTHER[axis], (0, -1, 1, 2)[k], first + W_SHARE * half, n1 + n2)
        sem = self.hand_sem + 4 * (n - SHARED_SETS[0]) + k
        return self.remote(sheet, sheet, sem, sem, self.twin)

    def helped(self, n, k):
        axis, first, n1, n2 = GATHER_SETS[n]
        axis, step = OTHER[axis], (0, -1, 1, 2)[k]
        src = self.sheet(self.gw, axis, step, first, n1 + n2)
        dst = self.sheet(self.w, axis, step, first - G_HELP + W_HELP, n1 + n2)
        sem = self.help_sem + 4 * (n - HELP_SETS[0]) + k
        return self.remote(src, dst, sem, sem, self.partner)

    def spread_sent(self, sets):
        for n in sets:
            for stage in range(4):
                for copy in self.spread(n, stage):
                    copy.wait_send()

    def spread_done(self):
        self.spread_sent(range(8))
        for n in SHARED_SETS:
            for k in range(4):
                self.handed(n, k, self.part).wait_send()

    def weight(self, first, count):
        return self.w[:, :, :, first : first + count].reshape(D, count)

    def heads_out(self, to):
        theirs = self.w.at[pl.ds(2 * (1 - self.core), 2), :, :, pl.ds(W_O, HALF)]
        return self.remote(theirs, self.out_columns(to), self.head_sem, self.head_sem, self.sibling)

    def heads_keep(self):
        own = self.w.at[pl.ds(2 * self.core, 2), :, :, pl.ds(W_O, HALF)]
        return self.local(own, self.out_columns(self.core), self.head_sem + 1)

    def out_columns(self, of):
        return self.of.at[:, :, :, columns(HALF * of, HALF)]

    def heads_start(self):
        self.heads_out(self.core).start()
        self.heads_keep().start()

    def vectors_in(self):
        vec = self.weight(W_VEC, 128).astype(F32).T
        self.vec[...] = vec[:8, :]

    def heads_wait(self):
        self.heads_keep().wait()
        self.heads_out(1 - self.core).wait_recv()
        self.heads_out(self.core).wait_send()

    def out_rows(self):
        return self.of[...].reshape(HALF, D)

    def swap(self, turn, i):
        rows, sem = rows_of(i), self.swap_sem + 2 * turn + i
        return self.remote(
            self.es.at[rows], self.er.at[turn % 2, rows], sem, sem, self.sibling
        )

    def mail_piece(self, i, half):
        return rows_of(i), pl.ds(pl.multiple_of(half * HALF, 128), HALF)

    def mail_send(self, i):
        piece, sem = self.mail_piece(i, self.core), self.mail_sem + i
        return self.remote(self.xin.at[piece], self.mail.at[piece], sem, sem, self.partner)

    def mail_wait(self, i):
        own, other = self.mail_piece(i, self.core), self.mail_piece(i, 1 - self.core)
        sem = self.mail_sem + 2 + i
        self.mail_send(i).wait_recv()
        copy = self.remote(self.mail.at[own], self.mail.at[own], sem, sem, self.sibling)
        copy.start()
        self.remote(self.mail.at[other], self.mail.at[other], sem, sem, self.sibling).wait_recv()
        copy.wait_send()

    def vec_row(self, n):
        return self.vec[n : n + 1, :]

    def vec_half(self, n):
        return self.vec[n : n + 1, pl.ds(pl.multiple_of(self.core * HALF, 128), HALF)]

    def masked(self, values, fill, hi):
        lane = lax.broadcasted_iota(jnp.int32, values.shape, 1)
        return jnp.where((lane >= 64) if hi else (lane < 64), values, fill)

    def attend(self, j):
        q2 = self.qkvt[:, HALF * j : HALF * j + 128]
        k2 = self.qkvt[:TOK, HALF * j + 128 : HALF * j + 256]
        v2t = self.qkvt[:TOK, HALF * j + 256 : HALF * j + 384].T
        ones = jnp.ones((16, TOK), BF16)
        mixed = []
        for hi in range(2):
            scores = dot(k2, self.masked(q2, jnp.zeros_like(q2), hi), NT)
            weights = jnp.exp(scores - jnp.max(scores, axis=0, keepdims=True)).astype(BF16)
            self.p[2 * j + hi] = weights
            made = dot(jnp.concatenate([v2t[64 * hi : 64 * hi + 64, :], ones], axis=0), weights)
            scale = 1.0 / made[64:65, :]
            self.linv[2 * j + hi : 2 * j + hi + 1, :] = scale
            mixed.append(made[:64, :] * scale)
        mixed = jnp.concatenate(mixed, axis=0).T
        self.mf[:, 128 * j : 128 * j + 128] = mixed
        self.m[self.core, :, 128 * j : 128 * j + 128] = mixed.astype(BF16)

    def normed(self, i, values, unit_ref, scale_ref, gain, shift):
        rows = rows_of(i)
        center, scale = center_rows(values)
        unit = center * scale
        unit_ref[rows, :] = unit.astype(BF16)
        scale_ref[rows, :] = scale
        return (unit * gain + shift).astype(BF16)

    def enter(self, i):
        rows = rows_of(i)
        values = self.xin[rows, :].astype(F32)
        self.abuf[rows, :] = self.normed(i, values, self.ua, self.sa, self.vec_row(0), self.vec_row(2))

    def project(self, i):
        rows = rows_of(i)
        made = dot(self.abuf[rows, :], self.weight(0, 3 * HALF))
        bias_q, bias_v = self.vec_half(3), self.vec_half(4)
        for j in range(3):
            at, own = HALF * j, slice(128 * j, 128 * j + 128)
            query = (made[:, at : at + 128] + bias_q[:, own]).astype(BF16) * BF16(SCALE)
            self.qkvt[rows, at : at + 128] = query
            self.qkvt[rows, at + 128 : at + 256] = made[:, at + 128 : at + 256].astype(BF16)
            self.qkvt[rows, at + 256 : at + 384] = (made[:, at + 256 : at + 384] + bias_v[:, own]).astype(BF16)

    def attended(self):
        self.es[...] = dot(self.m[self.core, :TOK, :], self.out_rows()).astype(BF16)

    def swapped(self, turn, i):
        self.swap(turn, i).wait()
        rows = rows_of(i)
        return self.es[rows, :].astype(F32) + self.er[turn % 2, rows, :].astype(F32)

    def widen(self, i):
        rows = rows_of(i)
        middle = self.xin[rows, :].astype(F32) + self.swapped(0, i) + self.vec_row(5)
        self.h[rows, :] = middle
        self.bbuf[rows, :] = self.normed(i, middle, self.ub, self.sb, self.vec_row(1), self.vec_row(6))
        for n in range(3):
            cols = slice(512 * n, 512 * n + 512)
            pre = dot(self.bbuf[rows, :], self.weight(W_U + 512 * n, 512)) + self.hbuf[0:1, cols]
            square = pre * pre
            soft = 0.5 + 0.5 * jnp.tanh(pre * (0.7978845608028654 + 0.035677408136300125 * square))
            made = pre * soft
            self.g[rows, cols] = made.astype(BF16)
            slope = made * (1.0 - soft) * (1.5957691216057308 + 0.21406444881780074 * square)
            self.gz[rows, cols] = (soft + slope).astype(BF16)

    def narrow(self, i):
        rows = rows_of(i)
        self.es[rows, :] = dot(self.g[rows, :], self.weight(W_V, FH), NT).astype(BF16)

    def rows_out(self):
        rows = lax.dot_general(self.sel[...], self.yb[...], TN, preferred_element_type=F32)
        self.chunks[...] = rows.astype(BF16).reshape(4, SLOTP, D)

        @pl.when(self.core == self.role)
        def _():
            for zd in range(4):
                self.push(*self.rows_push(zd))

    def leave(self, i):
        rows = rows_of(i)
        out = (self.h[rows, :] + self.swapped(1, i) + self.vec_row(7)).astype(BF16)

        @pl.when(self.role == 0)
        def _():
            self.xin[rows, :] = out
            self.mail_send(i).start()

        @pl.when(self.role == 1)
        def _():
            self.yb[rows, :] = out

    def perform(self, order):
        at = 0
        while at < len(order):
            end = at
            while end < len(order) and order[end][0] < PROJ:
                end += 1
            if end > at:

                @pl.when(self.role == 0)
                def _():
                    for item in order[at:end]:
                        self.step(*item)

            if end < len(order):
                self.step(*order[end])
            at = end + 1

    def step(self, name, n=0, stage=0):
        STEPS[name](self, n, stage)

    def do_A(self, n, stage):
        if stage:
            for copy in self.spread(n, stage - 1, True):
                copy.wait_recv()
        for copy in self.spread(n, stage):
            copy.start()

    def do_F(self, n, stage):
        for copy in self.spread(n, 3, True):
            copy.wait_recv()

    def do_Z(self, n, stage):
        for k in ((0,), (1, 2), (3,))[stage]:
            self.handed(n, k, self.part).start()

    def do_WZ(self, n, stage):
        for k in range(4):
            self.handed(n, k, 1 - self.part).wait_recv()

    def do_H(self, n, stage):
        for k in ((0,), (1, 2), (3,))[stage]:
            self.helped(n, k).start()

    def do_WH(self, n, stage):
        for n in HELP_SETS:
            for k in range(4):
                self.helped(n, k).wait_recv()

    def do_chunk(self, n, stage):
        self.chunk_wait()

    def do_vec(self, n, stage):
        self.vectors_in()

    def do_heads(self, n, stage):
        self.heads_start()

    def do_enter(self, n, stage):
        self.enter(0)
        self.enter(1)

    def do_proj(self, n, stage):
        for i in range(2):

            @pl.when(self.role == 1)
            def _():
                self.mail_wait(i)
                rows = rows_of(i)
                self.xin[rows, :] = self.mail[rows, :D]
                self.enter(i)

            self.project(i)
            if i == 0:

                @pl.when(self.role == 1)
                def _():
                    for item in GATHER_WAITS:
                        self.step(*item)
                    self.shrink_ahead()


    def do_at(self, n, stage):
        if self.turned:
            self.attend_back(n)
        else:
            self.attend(n)

    def do_out(self, n, stage):
        self.share(self.core).start()
        self.heads_wait()
        self.attended()
        for i in range(2):
            self.swap(0, i).start()

    def do_wide(self, n, stage):
        self.widen(n)

    def do_nar(self, n, stage):
        for i in range(2):
            self.narrow(i)
            self.swap(1, i).start()

        @pl.when(self.role == 1)
        def _():
            self.shrink_late()

        for i in range(2):
            self.leave(i)

    def share(self, of):
        block = self.m.at[of]
        return self.remote(block, block, self.share_sem, self.share_sem, self.sibling)

    def turn_over(self):
        self.spread_done()
        self.share(self.core).wait_send()
        self.share(1 - self.core).wait_recv()

        low, high = self.perm[:, :HALF], self.perm[:, HALF:]
        for cols in (slice(0, 512), slice(512, TOKP)):
            made = dot(low, self.m[0, cols, :], NT) + dot(high, self.m[1, cols, :], NT)
            self.mt_t[:, cols] = made.astype(BF16)
        self.turn(self.abuf, self.at_t)
        self.turn(self.bbuf, self.bt_t)

    def turn(self, ref, to):
        for cols in (slice(0, 512), slice(512, TOKP)):
            to[:, cols] = dot(self.perm[...], ref[cols, :], NT).astype(BF16)

    def put(self, first, count, value):
        self.gw[:, :, :, pl.ds(first, count)] = value.astype(BF16).reshape(4, 4, SHARD, count)

    def attend_back(self, j):
        lane = lax.broadcasted_iota(jnp.int32, (TOKP, 128), 1)
        cols, at = slice(128 * j, 128 * j + 128), HALF * j
        q2 = self.qkvt[:, at : at + 128]
        k2, v2 = self.qkvt[:TOK, at + 128 : at + 256], self.qkvt[:TOK, at + 256 : at + 384]
        scale = jnp.where(lane < 64, self.linv_t[:, 2 * j : 2 * j + 1], self.linv_t[:, 2 * j + 1 : 2 * j + 2])
        d2 = (self.dm[:, cols].astype(F32) * scale).astype(BF16)
        both = d2.astype(F32) * self.mf[:, cols]
        k2t, q2t, d2t = k2.T, q2.T, d2.T
        grads = [[], [], []]
        for hi in range(2):
            head = slice(64 * hi, 64 * hi + 64)
            inner = jnp.sum(self.masked(both, jnp.zeros_like(both), hi), axis=1, keepdims=True)
            high = inner.astype(BF16)
            rest = (inner - high.astype(F32)).astype(BF16)
            spare = 0 if hi else 64
            taken = jnp.where(lane == spare, -high, jnp.where(lane == spare + 1, -rest, jnp.zeros_like(high)))
            near = lax.broadcasted_iota(jnp.int32, (TOK, 128), 1) - spare
            fill = jnp.where((near == 0) | (near == 1), 1.0, 0.0).astype(BF16)
            grad_soft = dot(self.masked(v2, fill, hi), self.masked(d2, taken, hi), NT)
            soft = self.p[2 * j + hi]
            grad_score = (soft.astype(F32) * grad_soft).astype(BF16)
            grads[0].append(dot(k2t[head, :], grad_score) * SCALE)
            grads[1].append(dot(q2t[head, :], grad_score, NT))
            grads[2].append(dot(d2t[head, :], soft, NT))
        for t in range(3):
            grad = jnp.concatenate(grads[t], axis=0).T[:TOK].astype(BF16)
            self.dqkv[:TOK, at + 128 * t : at + 128 * t + 128] = grad

    def through(self, rows, cols, made):
        self.gz[rows, cols] = (made * self.gz[rows, cols].astype(F32)).astype(BF16)

    def shrink_ahead(self):
        @pl.loop(0, 3)
        def _(a):
            rows = pl.ds(pl.multiple_of(192 * a, 16), 192)
            for n in range(3):
                made = dot(self.dr[rows, :], self.weight(W_V + 512 * n, 512))
                self.gw[a, :, :, 512 * n : 512 * n + 512] = made.astype(BF16).reshape(4, SHARD, 512)

    def shrink_late(self):
        @pl.loop(0, 12)
        def _(k):
            rows = pl.ds(pl.multiple_of(SHARD * k, 16), SHARD)
            self.through(rows, slice(0, FH), self.gw[k // 4, lax.rem(k, 4), :, :FH].astype(F32))

    def shrink_back(self, i):
        rows = rows_of(i)
        grad = self.dr[rows, :]
        @pl.when(self.role == 0)
        def _():
            for n in range(3):
                cols = slice(512 * n, 512 * n + 512)
                self.through(rows, cols, dot(grad, self.weight(W_V + 512 * n, 512)))

        self.es[rows, :] = dot(self.gz[rows, :], self.weight(W_U, FH), NT).astype(BF16)
        self.swap(2, i).start()

    def middle_back(self, i):
        rows = rows_of(i)
        grad = self.swapped(2, i)
        unit = self.ub[rows, :].astype(F32)
        back = norm_back(grad, unit, self.sb[rows, :], self.vec_row(1))
        self.vsum[5:6, :] += jnp.sum(grad * unit, axis=0, keepdims=True)
        self.vsum[1:2, :] += jnp.sum(grad, axis=0, keepdims=True)
        back = back + self.dr[rows, :].astype(F32)
        self.h[rows, :] = back
        low = back.astype(BF16)
        self.mail[rows, :D] = low
        self.dm[rows, :] = dot(low, self.out_rows(), NT).astype(BF16)

    def project_back(self, i):
        rows = rows_of(i)
        self.es[rows, :] = dot(self.dqkv[rows, : 3 * HALF], self.weight(0, 3 * HALF), NT).astype(BF16)
        self.swap(3, i).start()

    def enter_back(self, i):
        rows = rows_of(i)
        grad = self.swapped(3, i)
        unit = self.ua[rows, :].astype(F32)
        back = norm_back(grad, unit, self.sa[rows, :], self.vec_row(0))
        self.vsum[4:5, :] += jnp.sum(grad * unit, axis=0, keepdims=True)
        self.vsum[3:4, :] += jnp.sum(grad, axis=0, keepdims=True)
        back = back + self.h[rows, :]

        low = back.astype(BF16)

        @pl.when(self.role == 0)
        def _():
            self.yb[rows, :] = low

        @pl.when(self.role == 1)
        def _():
            self.xin[rows, :] = low
            self.mail_send(i).start()

    def given(self, i):
        self.mail_wait(i)
        rows = rows_of(i)
        self.dr[rows, :] = self.mail[rows, :D]

    def grad_columns(self, left, right, first, to):
        self.put(to, 512, dot(left[...], right[:, columns(first, 512)]))

    def do_gVs(self, n, stage):
        self.grad_columns(self.dr_t, self.g, 0, 0)

    def do_gVw(self, n, stage):
        self.grad_columns(self.dr_t, self.g, V_SHARE * (1 + self.part), V_SHARE)

    def do_gVo(self, n, stage):
        self.grad_columns(self.dr_t, self.g, V_SHARE * (2 - self.part), 2 * V_SHARE)
        for k in range(2):
            self.pair(k).start()

    def pair(self, k):
        sem = self.pair_sem + k
        src = self.gw.at[:, :, :, pl.ds(2 * V_SHARE + 256 * k, 256)]
        return self.remote(src, self.pr.at[:, :, :, pl.ds(256 * k, 256)], sem, sem, self.twin)

    def do_PA(self, n, stage):
        self.pair(n).wait_recv()
        every, cols = slice(None), slice(V_SHARE + 256 * n, V_SHARE + 256 * n + 256)
        add_to(self.gw, (every, every, every, cols), self.pr[:, :, :, 256 * n : 256 * n + 256].astype(F32))

    def do_gU(self, n, stage):
        for t in ((0, 1), (2,))[n]:
            self.grad_columns(self.bt_t, self.gz, 512 * t, G_U + 512 * t)

    def do_gO(self, n, stage):
        self.grad_out()

    def do_gP(self, n, stage):
        self.grad_pair(n)

    def do_R(self, n, stage):
        self.sum_stage(n, stage)

    def do_D(self, n, stage):
        self.sums_start(n)

    def do_g1(self, n, stage):
        self.given(1)
        self.turn(self.dr, self.dr_t)

    def do_sh(self, n, stage):
        self.shrink_back(n)

    def do_mid(self, n, stage):
        self.middle_back(n)

    def do_pb(self, n, stage):
        self.project_back(n)

    def do_en(self, n, stage):
        self.enter_back(n)

    def do_rows(self, n, stage):
        self.rows_out()

    def column_sums(self):
        def sums(ref, first, count):
            return jnp.sum(ref[:TOK, first : first + count].astype(F32), axis=0, keepdims=True)

        self.vsum[2:3, :] = sums(self.dr, 0, D)
        self.vsum[0:1, :] = sums(self.mail, 0, D)
        self.hsum[...] = sums(self.gz, 0, FH)
        for j in range(3):
            self.qsum[:, 128 * j : 128 * j + 128] = sums(self.dqkv, HALF * j, 128)
            self.qsum[:, HALF + 128 * j : HALF + 128 * j + 128] = sums(self.dqkv, HALF * j + 256, 128)

    def do_smx(self, n, stage):
        self.column_sums()
        self.small_pack()
        self.small_start("x")

    def do_smy(self, n, stage):
        self.sy[self.y] = self.small_wait("x")
        self.small_start("y")

    def do_smz(self, n, stage):
        self.sp[...] = self.small_wait("y")
        for zd in range(4):
            self.push(*self.small_push(zd))

    def grad_out(self):
        half = pl.ds(pl.multiple_of(self.core * HALF, 128), 512)
        self.put(G_O, HALF, dot(self.mt_t[...], self.mail[:, half])[:, :HALF])

    def grad_pair(self, j):
        made = dot(self.at_t[...], self.dqkv[:, HALF * j : HALF * j + 512])
        self.put(G_P + HALF * j, HALF, made[:, :HALF])

    def backward(self):
        self.vsum[...] = jnp.zeros_like(self.vsum)
        self.linv_t[...] = self.linv[...].T

        @pl.when(self.role == 0)
        def _():
            self.turn_over()
            self.mail_send(0).wait_send()
            self.mail_send(1).wait_send()
            self.given(0)

        self.perform(BACKWARD_ORDER)

        @pl.when(self.role == 1)
        def _():
            self.turn_over()
            self.turn(self.dr, self.dr_t)
            for item in SUM_ORDER:
                self.step(*item)

    def sum_into(self, n, stage):
        _, _, n1, n2 = SCATTER_SETS[n]
        ref = getattr(self, "sum%d_%d" % (stage, n))
        return ref, (n1 + n2, n1 + n2) if stage % 2 else (n1, n2)

    def sum_got(self, n, stage, i):
        ref, counts = self.sum_into(n, stage)
        return ref[i, ..., : counts[i]].astype(F32)

    def sum_copies(self, n, stage):
        axis, c0, n1, _ = SCATTER_SETS[n]
        view = self.sheet if stage < 2 else self.line
        axis = axis if stage < 2 else OTHER[axis]
        sem = self.scatter_sem + 8 * n + 2 * stage
        ref, counts = self.sum_into(n, stage)
        copies = []
        for i, step in enumerate((1, -1)):
            if counts[i] == 0:
                continue
            if stage % 2 == 0:
                block = view(self.gw, axis, 2, c0 + n1 * i, counts[i])
            else:
                block = view(self.gw, axis, step, c0, counts[i])
            cols = pl.ds(0, counts[i])
            into = ref.at[i, :, :, cols] if stage < 2 else ref.at[i, :, cols]
            copies.append(self.remote(block, into, sem + i, sem + i, self.near(axis, step)))
        return copies

    def sum_index(self, n, stage, step, first, count):
        axis, c0, _, _ = SCATTER_SETS[n]
        axis = axis if stage < 2 else OTHER[axis]
        at, cols = self.at(axis, step), slice(c0 + first, c0 + first + count)
        every = slice(None)
        if stage < 2:
            return (every, at, every, cols) if axis == "x" else (at, every, every, cols)
        return (self.y, at, every, cols) if axis == "x" else (at, self.x, every, cols)

    def sum_stage(self, n, stage):
        _, c0, n1, n2 = SCATTER_SETS[n]
        if stage > 0:
            for copy in self.sum_copies(n, stage - 1):
                copy.wait()
        if stage in (1, 3):
            add_to(self.gw, self.sum_index(n, stage, 1, 0, n1), self.sum_got(n, stage - 1, 0))
            if n2:
                add_to(self.gw, self.sum_index(n, stage, -1, n1, n2), self.sum_got(n, stage - 1, 1))
        elif stage == 2:
            got = self.sum_got(n, 1, 0) + self.sum_got(n, 1, 1)
            add_to(self.gw, self.sum_index(n, 0, 0, 0, n1 + n2), got)
        elif stage == 4:
            got = self.sum_got(n, 3, 0) + self.sum_got(n, 3, 1)
            total = self.gw[self.sum_index(n, 3, 0, 0, n1 + n2)].astype(F32) + got
            self.fin[:, : n1 + n2] = total
            for zd in range(4):
                self.dist[zd, :12, c0 : c0 + n1 + n2] = self.fin[12 * zd : 12 * zd + 12, : n1 + n2].astype(BF16)
        if stage < 4:
            for copy in self.sum_copies(n, stage):
                copy.start()

    def small_pack(self):
        n = 0
        for ref, rows in ((self.qsum, 0), (self.vsum, 6), (self.hsum, 0)):
            if rows:
                for row in range(rows):
                    for t in range(3):
                        cols = pl.ds(pl.multiple_of(self.core * HALF + 128 * t, 128), 128)
                        self.sx[self.x, n : n + 1, :] = ref[row : row + 1, cols]
                        n += 1
            else:
                for t in range(ref.shape[1] // 128):
                    self.sx[self.x, n : n + 1, :] = ref[0:1, 128 * t : 128 * t + 128]
                    n += 1
        self.sx[self.x, n:, :] = jnp.zeros((40 - n, 128), F32)

    def small_copies(self, axis, incoming=False):
        ref, at, base = (self.sx, self.x, self.small_sem) if axis == "x" else (self.sy, self.y, self.small_sem + 3)
        copies = []
        for step in (1, 2, 3):
            block = ref.at[mod4(at - step) if incoming else at]
            copies.append(self.remote(block, block, base + step - 1, base + step - 1, self.near(axis, step)))
        return copies

    def small_start(self, axis):
        for copy in self.small_copies(axis):
            copy.start()

    def small_wait(self, axis):
        for copy in self.small_copies(axis, True):
            copy.wait_recv()
        for copy in self.small_copies(axis):
            copy.wait_send()
        ref = self.sx if axis == "x" else self.sy
        return ref[0] + ref[1] + ref[2] + ref[3]

    def push(self, here, src, dst, send, recv, device):
        @pl.when(here)
        def _():
            self.local(src, dst, recv).start()

        @pl.when(jnp.logical_not(here))
        def _():
            self.remote(src, dst, send, recv, device).start()

    def sent(self, here, src, dst, send, recv, device):
        @pl.when(jnp.logical_not(here))
        def _():
            self.remote(src, dst, send, recv, device).wait_send()

    def got(self, here, src, dst, recv):
        @pl.when(here)
        def _():
            self.local(src, dst, recv).wait()

        @pl.when(jnp.logical_not(here))
        def _():
            self.remote(src, dst, 0, recv, self.sibling).wait_recv()

    def sum_push(self, group, j):
        cols, sem = pl.ds(FH * group, (2 * V_SHARE, FH, FH)[group]), self.sums_sem + 4 * group
        here = (self.core == self.role) & (self.z == j)
        return (
            here,
            self.dist.at[j, :, cols],
            self.rd.at[self.part, self.core, :, cols],
            sem + j,
            sem + 2 * self.part + self.core,
            (self.role, j, self.f),
        )

    def small_push(self, zd):
        here = (self.core == self.role) & (self.z == zd)
        recv = self.smallz_sem + 2 * self.part + self.core
        return here, self.sp, self.sz.at[self.part, self.core], self.smallz_sem + zd, recv, (self.role, zd, self.f)

    def rows_push(self, zd):
        recv = self.rows_sem + self.image
        return self.z == zd, self.chunks.at[zd], self.rin.at[self.image], self.rows_sem + zd, recv, (self.core, zd, self.f)

    def sums_start(self, group):
        for j in range(4):
            self.push(*self.sum_push(group, j))

    def sums_wait(self, group):
        cols = pl.ds(FH * group, (2 * V_SHARE, FH, FH)[group])
        for p in range(2):
            for cc in range(2):
                here = (self.core == cc) & (self.z == 2 * self.core + p)
                self.got(
                    here,
                    self.dist.at[0, :, cols],
                    self.rd.at[p, cc, :, cols],
                    self.sums_sem + 4 * group + 2 * p + cc,
                )

    def store(self, ref, cc, at, first, count):
        cols = slice(first, first + count)
        total = (self.rd[0, cc, :, cols].astype(F32) + self.rd[1, cc, :, cols].astype(F32))[:12, :]
        ref[:, :, at : at + count] = total.reshape(12, 1, count)

    def store_share(self, ref, cc, p, at):
        total = self.rd[p, cc, :, V_SHARE : 2 * V_SHARE].astype(F32)[:12, :]
        ref[:, :, at : at + V_SHARE] = total.reshape(12, 1, V_SHARE)

    def vectors_out(self):
        for p in range(2):
            for cc in range(2):
                here = (self.core == cc) & (self.z == 2 * self.core + p)
                self.got(here, self.sp, self.sz.at[p, cc], self.smallz_sem + 2 * p + cc)
        for cc in range(2):
            total = self.sz[0, cc] + self.sz[1, cc]
            for row, item in enumerate((6, 7, 0, 2, 3, 4, 5, 1)):
                for t in range(3):
                    first = HALF * cc + 128 * t
                    self.table[row : row + 1, first : first + 128] = total[3 * item + t : 3 * item + t + 1, :]
            for t in range(12):
                first = FH * cc + 128 * t
                self.gh[0:1, first : first + 128] = total[24 + t : 25 + t, :]
        first = 12 * (16 * self.z + self.f)
        own = pltpu.roll(self.table[...], lax.rem(D - first, D), 1)[:, :12]
        self.gg[0] = own[0:2, :]
        self.gb[0] = own[2:6, :]
        self.gvb[0] = own[6:8, :]

    def run(self):
        for name, count in (
            ("chunk_sem", 4),
            ("shard_sem", 17),
            ("gather_sem", 96),
            ("hand_sem", 8),
            ("help_sem", 8),
            ("pair_sem", 2),
            ("head_sem", 2),
            ("perm_sem", 1),
            ("swap_sem", 8),
            ("mail_sem", 4),
            ("share_sem", 1),
            ("scatter_sem", 96),
            ("small_sem", 6),
            ("smallz_sem", 4),
            ("sums_sem", 12),
            ("rows_sem", 4),
        ):
            setattr(self, name, self.take(count))
        self.greet()
        self.prepare()
        self.greeted()
        self.shard_start()
        self.chunk_send()
        self.perm_copy().start()
        self.zero_tails()
        for group in range(4):
            self.shard_wait(group)

        @pl.when(self.role == 1)
        def _():
            self.shard_wait(4)
            self.shard_wait(5)
            for item in GATHER_ORDER:
                self.step(*item)

        self.perm_copy().wait()
        self.turned = False
        self.perform(FORWARD_ORDER)

        @pl.when(self.role == 1)
        def _():
            self.spread_sent(range(8, 12))
            for n in HELP_SETS:
                for k in range(4):
                    self.helped(n, k).wait_send()

        self.turned = True
        self.backward()
        self.sums_wait(1)
        for cc in range(2):
            self.store(self.gu, cc, FH * cc, G_U, FH)
        self.sums_wait(2)
        for cc in range(2):
            self.store(self.go, cc, HALF * cc, G_O, HALF)
            for j in range(3):
                for t in range(3):
                    self.store(self.gq, cc, D * t + HALF * cc + 128 * j, G_P + HALF * j + 128 * t, 128)
        self.vectors_out()
        for m in range(2):
            source = m + self.core * (3 - 2 * m)
            self.got(self.z == source, self.chunks.at[0], self.rin.at[m], self.rows_sem + m)
            self.bnd[m] = self.rin[m, :SLOT, :].astype(F32)
        self.sums_wait(0)
        for cc in range(2):
            self.store(self.gv, cc, FH * cc, 0, V_SHARE)
            for p in range(2):
                self.store_share(self.gv, cc, p, FH * cc + V_SHARE * (1 + p))
        for n in range(4):
            for group in range(3):
                self.sent(*self.sum_push(group, n))
            self.sent(*self.small_push(n))

        @pl.when(self.core == self.role)
        def _():
            for n in range(4):
                self.sent(*self.rows_push(n))

        for k in range(2):
            self.pair(k).wait_send()

        @pl.when(self.role == 1)
        def _():
            self.mail_send(0).wait_send()
            self.mail_send(1).wait_send()


STEPS = (
    Kernel.do_A,
    Kernel.do_F,
    Kernel.do_Z,
    Kernel.do_WZ,
    Kernel.do_H,
    Kernel.do_WH,
    Kernel.do_chunk,
    Kernel.do_vec,
    Kernel.do_heads,
    Kernel.do_enter,
    Kernel.do_gVs,
    Kernel.do_gVw,
    Kernel.do_gVo,
    Kernel.do_PA,
    Kernel.do_gU,
    Kernel.do_gO,
    Kernel.do_gP,
    Kernel.do_R,
    Kernel.do_D,
    Kernel.do_g1,
    Kernel.do_rows,
    Kernel.do_smx,
    Kernel.do_smy,
    Kernel.do_smz,
    Kernel.do_proj,
    Kernel.do_at,
    Kernel.do_out,
    Kernel.do_wide,
    Kernel.do_nar,
    Kernel.do_sh,
    Kernel.do_mid,
    Kernel.do_pb,
    Kernel.do_en,
)
IN_NAMES = ("edges", "lengths", "qkv", "outw", "up", "down", "gains", "biases", "hidden", "order")
OUT_SHAPES = {
    "bnd": ((2, SLOT, D), F32),
    "gq": ((12, 1, 3 * D), F32),
    "go": ((12, 1, D), F32),
    "gu": ((12, 1, FF), F32),
    "gv": ((12, 1, FF), F32),
    "gg": ((1, 2, 12), F32),
    "gb": ((1, 4, 12), F32),
    "gvb": ((1, 2, 12), F32),
    "gh": ((1, FF), F32),
}
SCRATCH = {
    "w": ((4, 4, SHARD, W_ALL), BF16),
    "gw": ((4, 4, SHARD, G_ALL), BF16),
    "of": ((2, 4, SHARD, D), BF16),
    "hbuf": ((8, FH), F32),
    "hsource": ((8, FF), F32),
    "square": ((128, 128), F32),
    "vshard": ((SHARD, 128), BF16),
    "sel": ((TOK, TOKP), BF16),
    "yb": ((TOK, D), BF16),
    "table": ((8, D), F32),
    "vec": ((8, D), F32),
    "chunks": ((4, SLOTP, D), BF16),
    "slabs": ((4, SLOT // 8, 8, D), BF16),
    "rin": ((2, SLOTP, D), BF16),
    "xin": ((TOK, D), BF16),
    "mail": ((TOKP, D + 128), BF16),
    "abuf": ((TOKP, D), BF16),
    "bbuf": ((TOKP, D), BF16),
    "ua": ((TOK, D), BF16),
    "ub": ((TOK, D), BF16),
    "sa": ((TOK, 1), F32),
    "sb": ((TOK, 1), F32),
    "perm": ((D, D), BF16),
    "at_t": ((D, TOKP), BF16),
    "bt_t": ((D, TOKP), BF16),
    "mt_t": ((D, TOKP), BF16),
    "dr_t": ((D, TOKP), BF16),
    "qkvt": ((TOKP, 3 * HALF), BF16),
    "linv": ((8, TOKP), F32),
    "linv_t": ((TOKP, 8), F32),
    "p": ((6, TOK, TOKP), BF16),
    "m": ((2, TOKP, HALF), BF16),
    "mf": ((TOKP, HALF), F32),
    "h": ((TOK, D), F32),
    "gz": ((TOKP, FH), BF16),
    "g": ((TOKP, FH), BF16),
    "dr": ((TOKP, D), BF16),
    "dm": ((TOKP, HALF), BF16),
    "dqkv": ((TOKP, 3 * HALF + 128), BF16),
    "es": ((TOK, D), BF16),
    "er": ((2, TOK, D), BF16),
    "vsum": ((8, D), F32),
    "hsum": ((1, FH), F32),
    "qsum": ((1, D), F32),
    "pr": ((4, 4, SHARD, V_SHARE), BF16),
    "fin": ((SHARD, 768), F32),
    "dist": ((4, 16, G_ALL), BF16),
    "rd": ((2, 2, 16, G_ALL), BF16),
    "sx": ((4, 40, 128), F32),
    "sy": ((4, 40, 128), F32),
    "sp": ((40, 128), F32),
    "sz": ((2, 2, 40, 128), F32),
}
for _n, (_, _, _n1, _n2) in enumerate(SCATTER_SETS):
    for _stage, _count in enumerate((max(_n1, _n2), _n1 + _n2) * 2):
        SCRATCH["sum%d_%d" % (_stage, _n)] = ((2,) + ((4,) if _stage < 2 else ()) + (SHARD, _count), BF16)
COPIES = 320


def body(*refs):
    names = IN_NAMES + tuple(OUT_SHAPES) + tuple(SCRATCH) + ("send", "recv")
    Kernel(dict(zip(names, refs))).run()


def row_order():
    order = np.arange(D).reshape(4, 16, 12).transpose(1, 0, 2).reshape(D)
    return np.eye(D, dtype=np.float32)[order]


def copy_body(*refs):
    count = len(OUT_SHAPES)
    for n in range(count):
        refs[count + n][...] = refs[n][...]


def per_device(
    edges, lengths, qkv_weight, out_weight, up_weight, down_weight, gains, biases, hidden_bias
):
    rows = edges.reshape(2, SLOT // 8, 8, D)
    vmem = pl.BlockSpec(memory_space=pltpu.VMEM)
    smem = pl.BlockSpec(memory_space=pltpu.SMEM)
    anywhere = pl.BlockSpec(memory_space=pl.ANY)
    made = pl.pallas_call(
        body,
        out_shape=[jax.ShapeDtypeStruct(*spec) for spec in OUT_SHAPES.values()],
        in_specs=[anywhere, smem] + [anywhere] * 4 + [vmem] * 3 + [anywhere],
        out_specs=[vmem] * len(OUT_SHAPES),
        scratch_shapes=[pltpu.VMEM(*spec) for spec in SCRATCH.values()]
        + [pltpu.SemaphoreType.DMA((COPIES,)), pltpu.SemaphoreType.DMA((COPIES,))],
        compiler_params=pltpu.CompilerParams(
            collective_id=0, has_side_effects=True, vmem_limit_bytes=VMEM_BYTES
        ),
    )(
        rows,
        lengths,
        qkv_weight,
        out_weight,
        up_weight,
        jnp.swapaxes(down_weight, 1, 2),
        gains,
        biases,
        hidden_bias,
        jnp.asarray(row_order(), BF16),
    )
    bnd, gq, go, gu, gv, gg, gb, gvb, gh = pl.pallas_call(
        copy_body,
        out_shape=[jax.ShapeDtypeStruct(*spec) for spec in OUT_SHAPES.values()],
        in_specs=[vmem] * len(OUT_SHAPES),
        out_specs=[vmem] * len(OUT_SHAPES),
    )(*made)
    return (
        bnd[None, :, None],
        gq.reshape(1, 12, 3 * D),
        go.reshape(1, 12, D),
        gu.reshape(1, 12, FF),
        jnp.transpose(gv, (1, 2, 0)),
        gg,
        gb,
        gvb,
        gh,
    )


def solution(mesh):
    in_specs = (
        P("section", None, "fsdp", "seq", None),
        P(),
        P("section", "fsdp", None),
        P("section", "fsdp", None),
        P("section", "fsdp", None),
        P("section", None, "fsdp"),
        P("section", None, "fsdp"),
        P("section", None, "fsdp"),
        P("section", None),
    )
    out_specs = (
        P("section", None, "fsdp", "seq", None),
        P("section", ("seq", "fsdp"), None),
        P("section", ("seq", "fsdp"), None),
        P("section", ("seq", "fsdp"), None),
        P("section", None, ("seq", "fsdp")),
        P("section", None, ("seq", "fsdp")),
        P("section", None, ("seq", "fsdp")),
        P("section", None, ("seq", "fsdp")),
        P("section", None),
    )
    return jax.shard_map(
        per_device, mesh=mesh, in_specs=in_specs, out_specs=out_specs, check_vma=False
    )
```
